128 devices in a mesh: row: 8 (over z, core), col: 16 (over y, x).
Axes of the slice: x: 4, y: 4, z: 4, core: 2. Of those that a mesh axis runs over, the one named last changes fastest.
Arguments:
- queries: bfloat16 [256, 1024], P(('row', 'col')), may hold values from -6 to 6
- lists: bfloat16 [256, 4096, 1024], P(('row', 'col')), may hold values from -6 to 6
- list_home: int32 [256], replicated, may hold values from 0 to 255, each once
- probes: int32 [256, 16], replicated, may hold values from 0 to 255, all different within a row; in each aligned block of 256 rows (0 to 255, 256 to 511, ...) at most 64 rows name the same one
- initials: bfloat16 [262144, 1024], P(('row', 'col')), may hold values from -6 to 6
- item_home: int32 [262144], replicated, may hold values from 0 to 262143, as said below
- cands: int32 [256, 100], replicated, may hold values from 0 to 262143, as said below
Outputs:
- mass: float32 [256, 16], P(('row', 'col'))
- rerank: float32 [256, 100], P(('row', 'col'))
The draws below stay inside these ranges and needn't reach their ends.
Inputs may be any that keep to these rules, and one draw needn't show every extreme that they name: `probes`: each row names 16 different lists; no list is named by more than 64 rows, a bound that some block reaches. `list_home`: each number once. `item_home`: each number once. In each aligned block of 2 rows, the stored rows item_home[cands] fall into no aligned block of 2048 stored rows more than 2 times, and into some such block exactly 2 times.
All inputs are finite; a program needn't handle non-finite values.
Results may differ from the reference program's by a relative error of at most 0.00045.
Values may be sent and summed in bfloat16 or wider, within the bound.
No kernel may reach another device: no remote copies, remote signals or barrier semaphores. Data moves between devices by JAX's collectives and lax.ppermute only.
A program may use at most 64 MiB of HBM per device.

```python
import math
import jax
import jax.numpy as jnp
import numpy as np
from jax import lax

D = 1024
NPROBE = 16
K = 100
LIST_ROWS = 4096
Q_DEV = 2
ITEMS_DEV = 2048
QUERIES = 256
NLISTS = 256
NITEMS = 262144
MOST = 64


def shared_layout(key):
    home_order = jax.random.permutation(jax.random.fold_in(key, 11), NITEMS).astype(jnp.int32)
    blocks = QUERIES // Q_DEV
    slot_count = Q_DEV * K
    spread = min(blocks, slot_count // 2)
    owner_keys = jax.random.split(jax.random.fold_in(key, 12), blocks)
    owner_perms = jax.vmap(lambda single: jax.random.permutation(single, blocks))(owner_keys).astype(jnp.int32)
    cycle = (jnp.arange(slot_count, dtype=jnp.int32) % spread).astype(jnp.int32)
    owners = jnp.take(owner_perms, cycle, axis=1).astype(jnp.int32)
    shuffle_keys = jax.random.split(jax.random.fold_in(key, 13), blocks)
    shuffles = jax.vmap(lambda single: jax.random.permutation(single, slot_count))(shuffle_keys).astype(jnp.int32)
    owners = jnp.take_along_axis(owners, shuffles, axis=1).astype(jnp.int32)
    offsets = jax.random.randint(jax.random.fold_in(key, 14), (blocks, slot_count), 0, ITEMS_DEV).astype(jnp.int32)
    stored_rows = (owners * ITEMS_DEV + offsets).reshape(-1).astype(jnp.int32)
    inverse = jnp.argsort(home_order).astype(jnp.int32)
    chosen_ids = jnp.take(inverse, stored_rows, axis=0).astype(jnp.int32)
    return (home_order, chosen_ids.reshape(QUERIES, K))


def draw_item_home(key, part):
    home_order, chosen_ids = shared_layout(key)
    return home_order


def draw_cands(key, part):
    home_order, chosen_ids = shared_layout(key)
    return chosen_ids


def level_of(key, shape, pieces, smallest, top_value):
    loudness, own = 1.0, jax.random.fold_in(key, 6)
    for dim, blocks in pieces:
        heights = jnp.exp(jax.random.uniform(jax.random.fold_in(own, dim), (blocks,), jnp.float32, smallest / len(pieces), top_value / len(pieces)))
        loudness = loudness * jnp.repeat(heights, shape[dim] // blocks).reshape([-1 if axis == dim else 1 for axis in range(len(shape))])
    return loudness


def shared_out(own_key, own, number, rows, amount, top, reach, slope):
    ranking = jax.random.permutation(own_key, amount)
    heavy_load, common = load_shares(amount, rows * top, reach, slope, True), load_shares(amount, rows * top, reach, slope, False)
    places = jnp.arange(amount)

    def named(tallies, turn):
        used = int((tallies > 0).sum())
        fixed = max(1, used // 4)
        moved = fixed + (places - fixed + turn * (used - fixed)) % max(1, amount - fixed)
        return jnp.zeros((amount,), jnp.int32).at[ranking[jnp.where(places < fixed, places, moved)]].set(jnp.asarray(tallies, jnp.int32))

    tallies = jnp.where(number % 4 == 0, named(heavy_load, number // 4), named(common, number - number // 4 - 1))
    mixed = jax.random.permutation(jax.random.fold_in(own, 3), amount)
    giver, receiver = mixed[0:amount // 2 * 2:2], mixed[1:amount // 2 * 2:2]
    margin = jnp.minimum(tallies[giver] - 1, reach - tallies[receiver]) // 2
    margin = jnp.where((giver == ranking[0]) | (receiver == ranking[0]) | (tallies[receiver] == 0), 0, jnp.maximum(margin, 0))
    moved = jax.random.randint(jax.random.fold_in(own, 4), (amount // 2,), 0, 1 << 20) % (margin + 1)
    tallies = tallies.at[giver].add(-moved).at[receiver].add(moved)
    members = jnp.searchsorted(jnp.cumsum(tallies), jnp.arange(rows * top), side="right").astype(jnp.int32)
    table = members.reshape(top, rows).T
    table = table[jax.random.permutation(jax.random.fold_in(own, 1), rows)]
    turn = jax.random.randint(jax.random.fold_in(own, 2), (rows, 1), 0, top)
    return jnp.take_along_axis(table, (jnp.arange(top)[None, :] + turn) % top, axis=1)


def load_shares(count, total, most, skew, full):
    weights = [(1 << 20) // math.isqrt(standing ** skew) + 1 for standing in range(1, count + 1)]
    largest = most if full else min(most, max(-(-total // count), total * weights[0] // sum(weights)))
    least = 1 if total - largest >= count - 1 else 0
    counts, spare = [largest] + [least] * (count - 1), total - largest - least * (count - 1)
    while spare > 0:
        movable = [i for i in range(1, count) if counts[i] < largest] or [i for i in range(1, count) if counts[i] < most]
        whole, left = sum([weights[i] for i in movable]), spare
        for i in movable:
            extra = min(most - counts[i], max(1, left * weights[i] // whole), spare)
            counts[i] = counts[i] + extra
            spare = spare - extra
    return np.array(counts)


def scatter_about(own_key, shape, scale, most, pieces=(), kind=jnp.bfloat16):
    level = level_of(own_key, shape, pieces, -0.22, 0.18) if pieces else 1.0
    array = jax.random.normal(own_key, shape, jnp.float32) * scale * level
    return jnp.minimum(jnp.maximum(array, -most), most).astype(kind)


def setup_inputs(seed: int = 0) -> dict:
    key_of = jax.random.split(jax.random.key(seed), 8)
    queries = scatter_about(key_of[0], (QUERIES, D), 1.0, 6.0, ((0, 128),))
    lists = scatter_about(key_of[1], (NLISTS, LIST_ROWS, D), 1.0, 6.0, ((0, 128),))
    list_home = jax.random.permutation(key_of[2], NLISTS).astype(jnp.int32)
    probes_keys = jax.random.split(jax.random.fold_in(key_of[3], 1), QUERIES // QUERIES)
    probes_turns = jax.random.permutation(jax.random.fold_in(key_of[3], 3), QUERIES // QUERIES)
    probes = jax.vmap(lambda own, number: shared_out(jax.random.fold_in(key_of[3], 2), own, number, QUERIES, NLISTS, NPROBE, MOST, 2))(probes_keys, probes_turns).reshape((QUERIES, NPROBE))
    initials = scatter_about(key_of[4], (NITEMS, D), 1.0, 6.0, ((0, 128),))
    item_home = draw_item_home(jax.random.fold_in(key_of[7], 71), 0)
    cands = draw_cands(jax.random.fold_in(key_of[7], 71), 0)
    return dict(queries=queries, lists=lists, list_home=list_home, probes=probes, initials=initials, item_home=item_home, cands=cands)


def list_stat(query_rows, list_matrix, factor):
    total_rows = query_rows.shape[0]
    width = query_rows.shape[1]
    block_rows = min(512, total_rows)
    shaped = query_rows.reshape(total_rows // block_rows, block_rows, width)

    def block_stat(segment):
        scores = lax.dot_general(segment, list_matrix, (((1,), (1,)), ((), ())), preferred_element_type=jnp.float32) * factor
        return lax.optimization_barrier(jnp.mean(jnp.square(jnp.maximum(scores, 0.0)), axis=1))
    return lax.map(block_stat, shaped).reshape(total_rows)

def reference(queries, lists, list_home, probes, initials, item_home, cands):
    factor = 1.0 / math.sqrt(D)
    stored = jnp.take(list_home, probes, axis=0).astype(jnp.int32)
    index_row = jnp.arange(QUERIES, dtype=jnp.int32)

    def visit(totals, list_index):
        hits = stored == list_index
        flagged = jnp.any(hits, axis=1)
        order_keys = jnp.where(flagged, 0, 1).astype(jnp.int32) * QUERIES + index_row
        chosen = jnp.argsort(order_keys)[:MOST].astype(jnp.int32)
        list_matrix = lax.dynamic_index_in_dim(lists, list_index, 0, keepdims=False)
        stats = list_stat(jnp.take(queries, chosen, axis=0), list_matrix, factor)
        weights = jnp.where(flagged[chosen], stats, jnp.float32(0.0))[:, None] * hits[chosen].astype(jnp.float32)
        return (totals.at[chosen].add(weights), None)
    mass, _ = lax.scan(visit, jnp.zeros((QUERIES, NPROBE), jnp.float32), jnp.arange(NLISTS, dtype=jnp.int32))
    homes = jnp.take(item_home, cands, axis=0).astype(jnp.int32)

    def score_query(packed):
        query_vec, home_row = packed
        picked = jnp.take(initials, home_row, axis=0)
        return jnp.dot(picked, query_vec, preferred_element_type=jnp.float32)
    rerank = lax.map(score_query, (queries, homes))
    return (mass, rerank)
```

```python
import math

import jax
import jax.numpy as jnp
from jax import lax
from jax.experimental import pallas as pl
from jax.experimental.pallas import tpu as pltpu
from jax.sharding import PartitionSpec as P

AXES = ("row", "col")
LANES = 128
CHUNK = 512


def pack_kernel(held_items, queries_ref, homes_ref, send_ref):
    rows, width = send_ref.shape[0], queries_ref.shape[1]
    queries = queries_ref[...].astype(jnp.float32)
    odd = lax.broadcasted_iota(jnp.int32, (rows, width), 0) % 2 == 1
    send_ref[:, :width] = jnp.where(odd, queries[1:2, :], queries[0:1, :]).astype(send_ref.dtype)
    homes = homes_ref[...]
    row = lax.broadcasted_iota(jnp.int32, (rows, LANES), 0)
    lane = lax.broadcasted_iota(jnp.int32, (rows, LANES), 1)
    home = jnp.where(row % 2 == 1, homes[1:2, :], homes[0:1, :])
    owned = home // held_items == row // 2
    key = (lane * held_items + home % held_items).astype(jnp.float32)
    big = float(LANES * held_items)
    first = jnp.min(jnp.where(owned, key, big), axis=1, keepdims=True)
    last = jnp.max(jnp.where(owned, key, -1.0), axis=1, keepdims=True)
    one = jnp.where(first < big, first.astype(jnp.int32) % held_items, -256)
    two = jnp.where(last > first, last.astype(jnp.int32) % held_items, -256)
    digits = jnp.where(
        lane == 0,
        one >> 8,
        jnp.where(lane == 1, one & 255, jnp.where(lane == 2, two >> 8, jnp.where(lane == 3, two & 255, 0))),
    )
    send_ref[:, width:] = digits.astype(jnp.float32).astype(send_ref.dtype)


def score_kernel(
    scale, got_ref, lists_ref, items_ref, out_ref, lists_v, items_v, list_sems, item_sems
):
    count, width = got_ref.shape[0], lists_ref.shape[2]
    held, list_rows = lists_ref.shape[0], lists_ref.shape[1]
    per_list = list_rows // CHUNK
    item_chunks = items_ref.shape[0] // CHUNK

    def list_copy(i, j):
        rows = pl.ds(pl.multiple_of(j * CHUNK, CHUNK), CHUNK)
        return pltpu.make_async_copy(lists_ref.at[i, rows], lists_v.at[i, rows], list_sems.at[i, j])

    def item_copy(j):
        rows = pl.ds(pl.multiple_of(j * CHUNK, CHUNK), CHUNK)
        return pltpu.make_async_copy(items_ref.at[rows], items_v.at[rows], item_sems.at[j])

    for i in range(held):
        for j in range(per_list):
            list_copy(i, j).start()
    for j in range(item_chunks):
        item_copy(j).start()

    queries = got_ref[:, :width]
    digits = jnp.transpose(got_ref[:, width:].astype(jnp.float32))
    one = (digits[0:1, :] * 256.0 + digits[1:2, :]).astype(jnp.int32)
    two = (digits[2:3, :] * 256.0 + digits[3:4, :]).astype(jnp.int32)

    def scores(block):
        return lax.dot_general(
            block, queries, (((1,), (1,)), ((), ())), preferred_element_type=jnp.float32
        )

    def fold(values):
        return jnp.sum(values.reshape(CHUNK // 8, 8, count), axis=0)

    zero = jnp.zeros((8, count), jnp.float32)
    results = []
    for i in range(held):

        def list_step(j, total, i=i):
            list_copy(i, j).wait()
            rows = pl.ds(pl.multiple_of(j * CHUNK, CHUNK), CHUNK)
            positive = jnp.maximum(scores(lists_v[i, rows, :]), 0.0)
            return total + fold(positive * positive)

        total = lax.fori_loop(0, per_list, list_step, zero)
        results.append(jnp.sum(total, axis=0, keepdims=True) * scale)

    def item_step(j, totals):
        item_copy(j).wait()
        rows = pl.ds(pl.multiple_of(j * CHUNK, CHUNK), CHUNK)
        found = scores(items_v[rows, :])
        index = lax.broadcasted_iota(jnp.int32, (CHUNK, count), 0) + j * CHUNK
        return (
            totals[0] + fold(jnp.where(index == one, found, 0.0)),
            totals[1] + fold(jnp.where(index == two, found, 0.0)),
        )

    for total in lax.fori_loop(0, item_chunks, item_step, (zero, zero)):
        results.append(jnp.sum(total, axis=0, keepdims=True))
    results.append(jnp.zeros((LANES - len(results), count), jnp.float32))
    out_ref[...] = jnp.transpose(jnp.concatenate(results, axis=0))


def place_kernel(held_items, held_lists, back_ref, homes_ref, stored_ref, mass_ref, rerank_ref):
    rows = back_ref.shape[0]
    per_query, probed = rerank_ref.shape[1], mass_ref.shape[1]
    back = back_ref[...]
    owner = homes_ref[...] // held_items
    stored = stored_ref[...]
    row = lax.broadcasted_iota(jnp.int32, (rows, LANES), 0)
    first = lax.broadcasted_iota(jnp.int32, (LANES, LANES), 0)
    second = lax.broadcasted_iota(jnp.int32, (LANES, LANES), 1)
    for a in range(2):
        own = owner[a : a + 1, :].astype(jnp.float32)
        down = jnp.sum(jnp.where(first == second, own, 0.0), axis=1, keepdims=True)
        earlier = jnp.where((down == own) & (first < second), 1.0, 0.0)
        rank = jnp.sum(earlier, axis=0, keepdims=True)
        value = jnp.where(rank > 0.5, back[:, held_lists + 1 : held_lists + 2], back[:, held_lists : held_lists + 1])
        mine = row == owner[a : a + 1, :] * 2 + a
        picked = jnp.sum(jnp.where(mine, value, 0.0), axis=0, keepdims=True)
        rerank_ref[a : a + 1, :] = picked[:, :per_query]
        place = stored[a : a + 1, :]
        value = jnp.where(place % held_lists == 1, back[:, 1:2], back[:, 0:1])
        mine = row == (place // held_lists) * 2 + a
        picked = jnp.sum(jnp.where(mine, value, 0.0), axis=0, keepdims=True)
        mass_ref[a : a + 1, :] = picked[:, :probed]


def local(queries, lists, list_home, probes, initials, item_home, cands):
    device = lax.axis_index(AXES)
    devices = lax.axis_size(AXES)
    mine, width = queries.shape
    held_lists, list_rows = lists.shape[0], lists.shape[1]
    held_items = initials.shape[0]
    per_query, probed = cands.shape[1], probes.shape[1]
    scale = 1.0 / (width * list_rows)

    own_cands = lax.dynamic_slice(cands, (device * mine, 0), (mine, per_query))
    own_probes = lax.dynamic_slice(probes, (device * mine, 0), (mine, probed))
    homes = item_home.at[own_cands].get(mode="promise_in_bounds")
    homes = jnp.pad(homes, ((0, 0), (0, LANES - per_query)), constant_values=-1)
    stored = list_home.at[own_probes].get(mode="promise_in_bounds")
    stored = jnp.pad(stored, ((0, 0), (0, LANES - probed)), constant_values=-1)

    send = pl.pallas_call(
        lambda *refs: pack_kernel(held_items, *refs),
        out_shape=jax.ShapeDtypeStruct((devices * mine, width + LANES), queries.dtype),
        name="pack",
    )(queries, homes)
    got = lax.all_to_all(send, AXES, 0, 0, tiled=True)
    results = pl.pallas_call(
        lambda *refs: score_kernel(scale, *refs),
        out_shape=jax.ShapeDtypeStruct((devices * mine, LANES), jnp.float32),
        in_specs=[
            pl.BlockSpec(memory_space=pltpu.VMEM),
            pl.BlockSpec(memory_space=pl.ANY),
            pl.BlockSpec(memory_space=pl.ANY),
        ],
        out_specs=pl.BlockSpec(memory_space=pltpu.VMEM),
        scratch_shapes=[
            pltpu.VMEM(lists.shape, lists.dtype),
            pltpu.VMEM(initials.shape, initials.dtype),
            pltpu.SemaphoreType.DMA((held_lists, list_rows // CHUNK)),
            pltpu.SemaphoreType.DMA((held_items // CHUNK,)),
        ],
        compiler_params=pltpu.CompilerParams(vmem_limit_bytes=40 * 1024 * 1024),
        cost_estimate=pl.CostEstimate(
            flops=2 * devices * mine * width * (held_lists * list_rows + held_items),
            bytes_accessed=2 * width * (held_lists * list_rows + held_items),
            transcendentals=0,
        ),
        name="score",
    )(got, lists, initials)
    back = lax.all_to_all(results, AXES, 0, 0, tiled=True)
    return pl.pallas_call(
        lambda *refs: place_kernel(held_items, held_lists, *refs),
        out_shape=(
            jax.ShapeDtypeStruct((mine, probed), jnp.float32),
            jax.ShapeDtypeStruct((mine, per_query), jnp.float32),
        ),
        name="place",
    )(back, homes, stored)


def solution(mesh):
    return jax.shard_map(
        local,
        mesh=mesh,
        in_specs=(P(AXES, None), P(AXES, None, None), P(), P(), P(AXES, None), P(), P()),
        out_specs=(P(AXES, None), P(AXES, None)),
        check_vma=False,
    )
```

```python
import math

import jax
import jax.numpy as jnp
from jax import lax
from jax.experimental import pallas as pl
from jax.experimental.pallas import tpu as pltpu
from jax.sharding import PartitionSpec as P

AXES = ("row", "col")
LANES = 128
WHOLE = pl.BlockSpec(memory_space=pltpu.VMEM)
CHUNK = 512


def column_block(axes, mine):
    column = lax.axis_index(axes) * mine
    return pl.ds(pl.multiple_of(column // LANES * LANES, LANES), LANES), column % LANES


def column_of(block, place):
    lane = lax.broadcasted_iota(jnp.int32, block.shape, 1)
    return jnp.sum(jnp.where(lane == place, block, 0).astype(jnp.float32), axis=1, keepdims=True).astype(jnp.int32)


def homes_of(table_v, cands_v, cands_s, rows_v, place):
    for k in range(cands_v.shape[0]):
        rows_v[k : k + 1, :] = table_v[pl.ds(cands_s[k, place] // LANES, 1), :]
    return column_of(rows_v[...], column_of(cands_v[...], place) % LANES)


def pack_kernel(held_items, axes, queries_ref, cands_ref, table_ref, send_ref, queries_v, table_v, cands_v, cands_s, rows_v, sems):
    devices, mine, width = send_ref.shape[0], queries_ref.shape[0], queries_ref.shape[1]
    per_query = cands_ref.shape[0]
    block, place = column_block(axes, mine)
    copies = [
        pltpu.make_async_copy(cands_ref.at[:, block], cands_s, sems.at[0]),
        pltpu.make_async_copy(cands_ref.at[:, block], cands_v, sems.at[1]),
        pltpu.make_async_copy(table_ref, table_v, sems.at[2]),
        pltpu.make_async_copy(queries_ref, queries_v, sems.at[3]),
    ]
    for copy in copies:
        copy.start()
    copies[3].wait()
    send_ref[:, :, :width] = jnp.broadcast_to(queries_v[...][None], (devices, mine, width))
    for copy in copies[:3]:
        copy.wait()
    lane = lax.broadcasted_iota(jnp.int32, (per_query, LANES), 1)
    order = lax.broadcasted_iota(jnp.int32, (per_query, LANES), 0)
    big = float(per_query * held_items)
    digits = []
    for a in range(mine):
        home = homes_of(table_v, cands_v, cands_s, rows_v, place + a)
        key = (order * held_items + home % held_items).astype(jnp.float32)
        owned = home // held_items == lane
        first = jnp.min(jnp.where(owned, key, big), axis=0, keepdims=True)
        last = jnp.max(jnp.where(owned, key, -1.0), axis=0, keepdims=True)
        one = jnp.where(first < big, first.astype(jnp.int32) % held_items, -256)
        two = jnp.where(last > first, last.astype(jnp.int32) % held_items, -256)
        digits += [one >> 8, one & 255, two >> 8, two & 255]
    digits = [digit.astype(jnp.float32) for digit in digits]
    digits.append(jnp.zeros((LANES - len(digits), LANES), jnp.float32))
    digits = jnp.transpose(jnp.concatenate(digits, axis=0)).astype(send_ref.dtype)
    send_ref[:, :, width:] = jnp.broadcast_to(digits[:, None, :], (devices, mine, LANES))


def lookup_kernel(axes, mine, cands_ref, table_ref, probes_ref, list_home_ref, info_ref, table_v, cands_v, probes_v, list_home_v, cands_s, rows_v, sems):
    block, place = column_block(axes, mine)
    copies = [
        pltpu.make_async_copy(cands_ref.at[:, block], cands_s, sems.at[0]),
        pltpu.make_async_copy(cands_ref.at[:, block], cands_v, sems.at[1]),
        pltpu.make_async_copy(table_ref, table_v, sems.at[2]),
        pltpu.make_async_copy(probes_ref.at[:, block], probes_v, sems.at[3]),
        pltpu.make_async_copy(list_home_ref, list_home_v, sems.at[4]),
    ]
    for copy in copies:
        copy.start()
    for copy in copies:
        copy.wait()
    columns = [homes_of(table_v, cands_v, cands_s, rows_v, place + a) for a in range(mine)]
    for a in range(mine):
        ids = column_of(probes_v[...], place + a)
        stored = jnp.zeros_like(ids)
        for row in range(list_home_v.shape[0]):
            spread = jnp.broadcast_to(list_home_v[row : row + 1, :], (ids.shape[0], LANES))
            stored = stored + jnp.where(ids // LANES == row, column_of(spread, ids % LANES), 0)
        columns.append(stored)
    lane = lax.broadcasted_iota(jnp.int32, (LANES, LANES), 1)
    both = jnp.full((LANES, LANES), -1.0, jnp.float32)
    for j, column in enumerate(columns):
        column = column.astype(jnp.float32)
        short = jnp.full((LANES - column.shape[0], 1), -1.0, jnp.float32)
        both = jnp.where(lane == j, jnp.concatenate([column, short], axis=0), both)
    info_ref[...] = jnp.transpose(both)[: info_ref.shape[0], :].astype(jnp.int32)


def score_kernel(scale, got_ref, lists_ref, items_ref, out_ref):
    width, held, list_rows = lists_ref.shape[2], lists_ref.shape[0], lists_ref.shape[1]
    count = got_ref.shape[0] * got_ref.shape[1]
    got = got_ref[...].reshape(count, got_ref.shape[2])
    queries = got[:, :width]
    digits = jnp.transpose(got[:, width:].astype(jnp.float32))
    odd = lax.broadcasted_iota(jnp.int32, (1, count), 1) % 2 == 1
    digits = jnp.where(odd, digits[4:8, :], digits[0:4, :])
    one = (digits[0:1, :] * 256.0 + digits[1:2, :]).astype(jnp.int32)
    two = (digits[2:3, :] * 256.0 + digits[3:4, :]).astype(jnp.int32)

    def scores(block):
        return lax.dot_general(
            block, queries, (((1,), (1,)), ((), ())), preferred_element_type=jnp.float32
        )

    def fold(values):
        return jnp.sum(values.reshape(CHUNK // 8, 8, count), axis=0)

    results = []
    for i in range(held):
        total = jnp.zeros((8, count), jnp.float32)
        for start in range(0, list_rows, CHUNK):
            positive = jnp.maximum(scores(lists_ref[i, start : start + CHUNK, :]), 0.0)
            total = total + fold(positive * positive)
        results.append(jnp.sum(total, axis=0, keepdims=True) * scale)
    first = second = jnp.zeros((8, count), jnp.float32)
    for start in range(0, items_ref.shape[0], CHUNK):
        found = scores(items_ref[start : start + CHUNK, :])
        index = lax.broadcasted_iota(jnp.int32, (CHUNK, count), 0) + start
        first = first + fold(jnp.where(index == one, found, 0.0))
        second = second + fold(jnp.where(index == two, found, 0.0))
    results.append(jnp.sum(first, axis=0, keepdims=True))
    results.append(jnp.sum(second, axis=0, keepdims=True))
    results.append(jnp.zeros((LANES - len(results), count), jnp.float32))
    out_ref[...] = jnp.transpose(jnp.concatenate(results, axis=0))


def in_vmem(array):
    return pltpu.with_memory_space_constraint(array, pltpu.VMEM)


def in_hbm(array):
    return pltpu.with_memory_space_constraint(array, pltpu.HBM)


def place_kernel(held_items, held_lists, back_ref, info_ref, mass_ref, rerank_ref):
    rows = back_ref.shape[0]
    per_query, probed = rerank_ref.shape[1], mass_ref.shape[1]
    back = back_ref[...]
    owner = info_ref[0:2, :] // held_items
    stored = info_ref[2:4, :]
    row = lax.broadcasted_iota(jnp.int32, (rows, LANES), 0)
    first = lax.broadcasted_iota(jnp.int32, (LANES, LANES), 0)
    second = lax.broadcasted_iota(jnp.int32, (LANES, LANES), 1)
    for a in range(2):
        own = owner[a : a + 1, :].astype(jnp.float32)
        down = jnp.sum(jnp.where(first == second, own, 0.0), axis=1, keepdims=True)
        earlier = jnp.where((down == own) & (first < second), 1.0, 0.0)
        rank = jnp.sum(earlier, axis=0, keepdims=True)
        value = jnp.where(rank > 0.5, back[:, held_lists + 1 : held_lists + 2], back[:, held_lists : held_lists + 1])
        mine = row == owner[a : a + 1, :] * 2 + a
        picked = jnp.sum(jnp.where(mine, value, 0.0), axis=0, keepdims=True)
        rerank_ref[a : a + 1, :] = picked[:, :per_query]
        place = stored[a : a + 1, :]
        value = jnp.where(place % held_lists == 1, back[:, 1:2], back[:, 0:1])
        mine = row == (place // held_lists) * 2 + a
        picked = jnp.sum(jnp.where(mine, value, 0.0), axis=0, keepdims=True)
        mass_ref[a : a + 1, :] = picked[:, :probed]


def local(queries, lists, list_home, probes, initials, item_home, cands):
    devices = lax.axis_size(AXES)
    mine, width = queries.shape
    held_lists, list_rows = lists.shape[0], lists.shape[1]
    held_items = initials.shape[0]
    per_query, probed = cands.shape[1], probes.shape[1]
    scale = 1.0 / (width * list_rows)

    table = item_home.reshape(-1, LANES)
    send = pl.pallas_call(
        lambda *refs: pack_kernel(held_items, AXES, *refs),
        out_shape=pltpu.VMEM((devices, mine, width + LANES), queries.dtype),
        in_specs=[pl.BlockSpec(memory_space=pltpu.HBM)] * 3,
        out_specs=WHOLE,
        scratch_shapes=[
            pltpu.VMEM(queries.shape, queries.dtype),
            pltpu.VMEM((item_home.shape[0] // LANES, LANES), jnp.int32),
            pltpu.VMEM((per_query, LANES), jnp.int32),
            pltpu.SMEM((per_query, LANES), jnp.int32),
            pltpu.VMEM((per_query, LANES), jnp.int32),
            pltpu.SemaphoreType.DMA((4,)),
        ],
        compiler_params=pltpu.CompilerParams(vmem_limit_bytes=4 * 1024 * 1024),
        cost_estimate=pl.CostEstimate(flops=1<<36, bytes_accessed=1<<28, transcendentals=0),
        name="pack",
    )(in_hbm(queries), in_hbm(cands.T), in_hbm(table))
    got = lax.all_to_all(send, AXES, 0, 0, tiled=True)
    results = pl.pallas_call(
        lambda *refs: score_kernel(scale, *refs),
        out_shape=pltpu.VMEM((devices * mine, LANES), jnp.float32),
        in_specs=[WHOLE] * 3,
        out_specs=WHOLE,
        compiler_params=pltpu.CompilerParams(vmem_limit_bytes=16 * 1024 * 1024),
        cost_estimate=pl.CostEstimate(
            flops=2 * devices * mine * width * (held_lists * list_rows + held_items),
            bytes_accessed=2 * width * (held_lists * list_rows + held_items),
            transcendentals=0,
        ),
        name="score",
    )(in_vmem(got), in_vmem(lists), in_vmem(initials))
    results, table, late_cands, late_probes, homes = lax.optimization_barrier(
        (results, table, cands.T, probes.T, list_home.reshape(-1, LANES))
    )
    info = pl.pallas_call(
        lambda *refs: lookup_kernel(AXES, mine, *refs),
        out_shape=pltpu.VMEM((8, LANES), jnp.int32),
        in_specs=[pl.BlockSpec(memory_space=pltpu.HBM)] * 4,
        out_specs=WHOLE,
        scratch_shapes=[
            pltpu.VMEM(table.shape, jnp.int32),
            pltpu.VMEM((per_query, LANES), jnp.int32),
            pltpu.VMEM((probed, LANES), jnp.int32),
            pltpu.VMEM(homes.shape, jnp.int32),
            pltpu.SMEM((per_query, LANES), jnp.int32),
            pltpu.VMEM((per_query, LANES), jnp.int32),
            pltpu.SemaphoreType.DMA((5,)),
        ],
        compiler_params=pltpu.CompilerParams(vmem_limit_bytes=4 * 1024 * 1024),
        cost_estimate=pl.CostEstimate(flops=0, bytes_accessed=2 * 1024 * 1024, transcendentals=0),
        name="lookup",
    )(in_hbm(late_cands), in_hbm(table), in_hbm(late_probes), in_hbm(homes))
    back = lax.all_to_all(results, AXES, 0, 0, tiled=True)
    return pl.pallas_call(
        lambda *refs: place_kernel(held_items, held_lists, *refs),
        out_shape=(
            jax.ShapeDtypeStruct((mine, probed), jnp.float32),
            jax.ShapeDtypeStruct((mine, per_query), jnp.float32),
        ),
        name="place",
    )(in_vmem(back), in_vmem(info))


def solution(mesh):
    return jax.shard_map(
        local,
        mesh=mesh,
        in_specs=(P(AXES, None), P(AXES, None, None), P(), P(), P(AXES, None), P(), P()),
        out_specs=(P(AXES, None), P(AXES, None)),
        check_vma=False,
    )
```

```python
import math

import jax
import jax.numpy as jnp
from jax import lax
from jax.experimental import pallas as pl
from jax.experimental.pallas import tpu as pltpu
from jax.sharding import PartitionSpec as P

AXES = ("row", "col")
LANES = 128
WHOLE = pl.BlockSpec(memory_space=pltpu.VMEM)
CHUNK = 1024
EARLY = 3072


def column_block(axes, mine):
    column = lax.axis_index(axes) * mine
    start = pl.multiple_of((column >> 7) * LANES, LANES)
    return pl.ds(start, LANES), column & (LANES - 1)


def column_of(block, place):
    lane = lax.broadcasted_iota(jnp.int32, block.shape, 1)
    return jnp.sum(jnp.where(lane == place, block, 0).astype(jnp.float32), axis=1, keepdims=True).astype(jnp.int32)


def homes_of(table_v, cands_v, cands_s, rows_v, place):
    for k in range(cands_v.shape[0]):
        rows_v[k : k + 1, :] = table_v[pl.ds(cands_s[k, place] >> 7, 1), :]
    return column_of(rows_v[...], column_of(cands_v[...], place) & (LANES - 1))


def pack_kernel(held_items, axes, run, queries_ref, cands_ref, table_ref, send_ref, queries_v, table_v, cands_v, cands_s, rows_v, sems):
    devices, mine, width = send_ref.shape[0], queries_ref.shape[0], queries_ref.shape[1]
    per_query = cands_ref.shape[0]
    block, place = column_block(axes, mine)
    copies = [
        pltpu.make_async_copy(cands_ref.at[:, block], cands_s, sems.at[0]),
        pltpu.make_async_copy(cands_ref.at[:, block], cands_v, sems.at[1]),
        pltpu.make_async_copy(table_ref, table_v, sems.at[2]),
        pltpu.make_async_copy(queries_ref, queries_v, sems.at[3]),
    ]
    for copy in copies:
        copy.start()
    copies[3].wait()
    half = width // 2
    for start in range(0, devices, run):
        part = start // run % 2 * half
        send_ref[start : start + run, :, :half] = jnp.broadcast_to(queries_v[:, part : part + half][None], (run, mine, half))
    for copy in copies[:3]:
        copy.wait()
    lane = lax.broadcasted_iota(jnp.int32, (per_query, LANES), 1)
    order = lax.broadcasted_iota(jnp.int32, (per_query, LANES), 0)
    big = float(per_query * held_items)
    shift = held_items.bit_length() - 1
    digits = []
    for a in range(mine):
        home = homes_of(table_v, cands_v, cands_s, rows_v.at[a], place + a)
        key = (order * held_items + (home & (held_items - 1))).astype(jnp.float32)
        owned = home >> shift == lane
        first = jnp.min(jnp.where(owned, key, big), axis=0, keepdims=True)
        last = jnp.max(jnp.where(owned, key, -1.0), axis=0, keepdims=True)
        one = jnp.where(first < big, first.astype(jnp.int32) & (held_items - 1), -256)
        two = jnp.where(last > first, last.astype(jnp.int32) & (held_items - 1), -256)
        digits += [one >> 8, one & 255, two >> 8, two & 255]
    digits = [digit.astype(jnp.float32) for digit in digits]
    digits.append(jnp.zeros((LANES - len(digits), LANES), jnp.float32))
    digits = jnp.transpose(jnp.concatenate(digits, axis=0)).astype(send_ref.dtype)
    send_ref[:, :, half:] = jnp.broadcast_to(digits[:, None, :], (devices, mine, LANES))


def lookup_kernel(axes, mine, cands_ref, table_ref, probes_ref, list_home_ref, info_ref, table_v, cands_v, probes_v, list_home_v, cands_s, rows_v, sems):
    block, place = column_block(axes, mine)
    copies = [
        pltpu.make_async_copy(cands_ref.at[:, block], cands_s, sems.at[0]),
        pltpu.make_async_copy(cands_ref.at[:, block], cands_v, sems.at[1]),
        pltpu.make_async_copy(table_ref, table_v, sems.at[2]),
        pltpu.make_async_copy(probes_ref.at[:, block], probes_v, sems.at[3]),
        pltpu.make_async_copy(list_home_ref, list_home_v, sems.at[4]),
    ]
    for copy in copies:
        copy.start()
    for copy in copies:
        copy.wait()
    columns = [homes_of(table_v, cands_v, cands_s, rows_v.at[a], place + a) for a in range(mine)]
    for a in range(mine):
        ids = column_of(probes_v[...], place + a)
        stored = jnp.zeros_like(ids)
        for row in range(list_home_v.shape[0]):
            spread = jnp.broadcast_to(list_home_v[row : row + 1, :], (ids.shape[0], LANES))
            stored = stored + jnp.where(ids >> 7 == row, column_of(spread, ids & (LANES - 1)), 0)
        columns.append(stored)
    lane = lax.broadcasted_iota(jnp.int32, (LANES, LANES), 1)
    both = jnp.full((LANES, LANES), -1.0, jnp.float32)
    for j, column in enumerate(columns):
        column = column.astype(jnp.float32)
        short = jnp.full((LANES - column.shape[0], 1), -1.0, jnp.float32)
        both = jnp.where(lane == j, jnp.concatenate([column, short], axis=0), both)
    info_ref[...] = jnp.transpose(both)[: info_ref.shape[0], :].astype(jnp.int32)


def scores(block, queries):
    return lax.dot_general(block, queries, (((1,), (1,)), ((), ())), preferred_element_type=jnp.float32)


def early_kernel(got_ref, lists_ref, items_ref, part_ref):
    count, half = got_ref.shape[0] * got_ref.shape[1], lists_ref.shape[2] // 2
    mine = got_ref[...].reshape(count, got_ref.shape[2])[:, :half]
    own = pl.ds(pl.multiple_of((lax.axis_index("row") & 1) * half, half), half)
    held_items = items_ref.shape[0]
    for start in range(0, held_items, CHUNK):
        part_ref[start : start + CHUNK, :] = scores(items_ref[start : start + CHUNK, own], mine)
    for start in range(0, EARLY, CHUNK):
        to = slice(held_items + start, held_items + start + CHUNK)
        part_ref[to, :] = scores(lists_ref[0, start : start + CHUNK, own], mine)


def score_kernel(scale, got_ref, other_ref, part_ref, lists_ref, items_ref, out_ref, wide_ref):
    width, held, list_rows = lists_ref.shape[2], lists_ref.shape[0], lists_ref.shape[1]
    count = got_ref.shape[0] * got_ref.shape[1]
    got = got_ref[...].reshape(count, got_ref.shape[2])
    other = other_ref[...].reshape(got.shape)
    half = width // 2
    mine, theirs = got[:, :half], other[:, :half]
    core = lax.axis_index("row") & 1
    queries = jnp.concatenate([jnp.where(core == 0, mine, theirs), jnp.where(core == 0, theirs, mine)], axis=1)
    rest = pl.ds(pl.multiple_of((1 - core) * half, half), half)
    digits = jnp.transpose(got[:, half:].astype(jnp.float32))
    odd = lax.broadcasted_iota(jnp.int32, (1, count), 1) & 1 == 1
    digits = jnp.where(odd, digits[4:8, :], digits[0:4, :])
    one = (digits[0:1, :] * 256.0 + digits[1:2, :]).astype(jnp.int32)
    two = (digits[2:3, :] * 256.0 + digits[3:4, :]).astype(jnp.int32)

    def fold(values):
        return jnp.sum(values.reshape(CHUNK // 8, 8, count), axis=0)

    results = []
    for i in range(held):
        total = jnp.zeros((8, count), jnp.float32)
        for start in range(0, list_rows, CHUNK):
            rows = slice(start, start + CHUNK)
            if i == 0 and start < EARLY:
                done = slice(items_ref.shape[0] + start, items_ref.shape[0] + start + CHUNK)
                found = part_ref[done, :] + scores(lists_ref[i, rows, rest], theirs)
            else:
                found = scores(lists_ref[i, rows, :], queries)
            positive = jnp.maximum(found, 0.0)
            total = total + fold(positive * positive)
        results.append(jnp.sum(total, axis=0, keepdims=True) * scale)
    first = second = jnp.zeros((8, count), jnp.float32)
    for start in range(0, items_ref.shape[0], CHUNK):
        rows = slice(start, start + CHUNK)
        found = part_ref[rows, :] + scores(items_ref[rows, rest], theirs)
        index = lax.broadcasted_iota(jnp.int32, (CHUNK, count), 0) + start
        first = first + fold(jnp.where(index == one, found, 0.0))
        second = second + fold(jnp.where(index == two, found, 0.0))
    results.append(jnp.sum(first, axis=0, keepdims=True))
    results.append(jnp.sum(second, axis=0, keepdims=True))
    results = jnp.concatenate(results, axis=0)
    results = jnp.concatenate([results, pltpu.roll(results, count - 1, 1)], axis=0)
    results = jnp.concatenate([results, jnp.zeros((LANES - results.shape[0], count), jnp.float32)], axis=0)
    wide_ref[...] = jnp.transpose(results)
    out_ref[...] = wide_ref[pl.ds(0, out_ref.shape[0], stride=2), :]


def in_vmem(array):
    return pltpu.with_memory_space_constraint(array, pltpu.VMEM)


def in_hbm(array):
    return pltpu.with_memory_space_constraint(array, pltpu.HBM)


def place_kernel(held_items, held_lists, back_ref, info_ref, mass_ref, rerank_ref):
    rows = back_ref.shape[0]
    per_query, probed = rerank_ref.shape[1], mass_ref.shape[1]
    back = back_ref[...]
    owner = info_ref[0:2, :] >> (held_items.bit_length() - 1)
    stored = info_ref[2:4, :]
    row = lax.broadcasted_iota(jnp.int32, (rows, LANES), 0)
    first = lax.broadcasted_iota(jnp.int32, (LANES, LANES), 0)
    second = lax.broadcasted_iota(jnp.int32, (LANES, LANES), 1)
    for a in range(2):
        own = owner[a : a + 1, :].astype(jnp.float32)
        down = jnp.sum(jnp.where(first == second, own, 0.0), axis=1, keepdims=True)
        earlier = jnp.where((down == own) & (first < second), 1.0, 0.0)
        rank = jnp.sum(earlier, axis=0, keepdims=True)
        at = a * (held_lists + 2)
        value = jnp.where(rank > 0.5, back[:, at + held_lists + 1 : at + held_lists + 2], back[:, at + held_lists : at + held_lists + 1])
        picked = jnp.sum(jnp.where(row == owner[a : a + 1, :], value, 0.0), axis=0, keepdims=True)
        rerank_ref[a : a + 1, :] = picked[:, :per_query]
        place = stored[a : a + 1, :]
        value = jnp.where(place & 1 == 1, back[:, at + 1 : at + 2], back[:, at : at + 1])
        picked = jnp.sum(jnp.where(row == place >> 1, value, 0.0), axis=0, keepdims=True)
        mass_ref[a : a + 1, :] = picked[:, :probed]


def local(queries, lists, list_home, probes, initials, item_home, cands):
    devices = lax.axis_size(AXES)
    mine, width = queries.shape
    held_lists, list_rows = lists.shape[0], lists.shape[1]
    held_items = initials.shape[0]
    per_query, probed = cands.shape[1], probes.shape[1]
    scale = 1.0 / (width * list_rows)

    run = lax.axis_size("col")
    table = item_home.reshape(-1, LANES)
    send = pl.pallas_call(
        lambda *refs: pack_kernel(held_items, AXES, run, *refs),
        out_shape=pltpu.VMEM((devices, mine, width // 2 + LANES), queries.dtype),
        in_specs=[pl.BlockSpec(memory_space=pltpu.HBM)] * 3,
        out_specs=WHOLE,
        scratch_shapes=[
            pltpu.VMEM(queries.shape, queries.dtype),
            pltpu.VMEM((item_home.shape[0] // LANES, LANES), jnp.int32),
            pltpu.VMEM((per_query, LANES), jnp.int32),
            pltpu.SMEM((per_query, LANES), jnp.int32),
            pltpu.VMEM((mine, per_query, LANES), jnp.int32),
            pltpu.SemaphoreType.DMA((4,)),
        ],
        compiler_params=pltpu.CompilerParams(vmem_limit_bytes=4 * 1024 * 1024),
        cost_estimate=pl.CostEstimate(flops=1<<36, bytes_accessed=1<<28, transcendentals=0),
        name="pack",
    )(in_hbm(queries), in_hbm(cands.T), in_hbm(table))
    got = lax.all_to_all(send, AXES, 0, 0, tiled=True)
    pairs = [(i, i ^ 1) for i in range(lax.axis_size("row"))]
    other = lax.ppermute(got, "row", pairs)
    part = pl.pallas_call(
        early_kernel,
        out_shape=pltpu.VMEM((held_items + EARLY, devices * mine), jnp.float32),
        in_specs=[WHOLE] * 3,
        out_specs=WHOLE,
        compiler_params=pltpu.CompilerParams(vmem_limit_bytes=8 * 1024 * 1024),
        cost_estimate=pl.CostEstimate(
            flops=devices * mine * width * (held_items + EARLY),
            bytes_accessed=width * (held_items + EARLY), transcendentals=0,
        ),
        name="early",
    )(in_vmem(got), in_vmem(lists), in_vmem(initials))
    results = pl.pallas_call(
        lambda *refs: score_kernel(scale, *refs),
        out_shape=pltpu.VMEM((devices, LANES), jnp.float32),
        scratch_shapes=[pltpu.VMEM((devices * mine, LANES), jnp.float32)],
        in_specs=[WHOLE] * 5,
        out_specs=WHOLE,
        compiler_params=pltpu.CompilerParams(vmem_limit_bytes=16 * 1024 * 1024),
        cost_estimate=pl.CostEstimate(
            flops=2 * devices * mine * width * (held_lists * list_rows + held_items),
            bytes_accessed=2 * width * (held_lists * list_rows + held_items),
            transcendentals=0,
        ),
        name="score",
    )(in_vmem(got), in_vmem(other), in_vmem(part), in_vmem(lists), in_vmem(initials))
    results, table, late_cands, late_probes, homes = lax.optimization_barrier(
        (results, table, cands.T, probes.T, list_home.reshape(-1, LANES))
    )
    info = pl.pallas_call(
        lambda *refs: lookup_kernel(AXES, mine, *refs),
        out_shape=pltpu.VMEM((8, LANES), jnp.int32),
        in_specs=[pl.BlockSpec(memory_space=pltpu.HBM)] * 4,
        out_specs=WHOLE,
        scratch_shapes=[
            pltpu.VMEM(table.shape, jnp.int32),
            pltpu.VMEM((per_query, LANES), jnp.int32),
            pltpu.VMEM((probed, LANES), jnp.int32),
            pltpu.VMEM(homes.shape, jnp.int32),
            pltpu.SMEM((per_query, LANES), jnp.int32),
            pltpu.VMEM((mine, per_query, LANES), jnp.int32),
            pltpu.SemaphoreType.DMA((5,)),
        ],
        compiler_params=pltpu.CompilerParams(vmem_limit_bytes=4 * 1024 * 1024),
        cost_estimate=pl.CostEstimate(flops=0, bytes_accessed=2 * 1024 * 1024, transcendentals=0),
        name="lookup",
    )(in_hbm(late_cands), in_hbm(table), in_hbm(late_probes), in_hbm(homes))
    back = lax.all_to_all(results[:, None, :], AXES, 0, 0, tiled=True)[:, 0, :]
    return pl.pallas_call(
        lambda *refs: place_kernel(held_items, held_lists, *refs),
        out_shape=(
            jax.ShapeDtypeStruct((mine, probed), jnp.float32),
            jax.ShapeDtypeStruct((mine, per_query), jnp.float32),
        ),
        name="place",
    )(in_vmem(back), in_vmem(info))


def solution(mesh):
    return jax.shard_map(
        local,
        mesh=mesh,
        in_specs=(P(AXES, None), P(AXES, None, None), P(), P(), P(AXES, None), P(), P()),
        out_specs=(P(AXES, None), P(AXES, None)),
        check_vma=False,
    )
```

```python
import math

import jax
import jax.numpy as jnp
from jax import lax
from jax.experimental import pallas as pl
from jax.experimental.pallas import tpu as pltpu
from jax.sharding import PartitionSpec as P

AXES = ("row", "col")
LANES = 128
WHOLE = pl.BlockSpec(memory_space=pltpu.VMEM)
CHUNK = 1024
EARLY = 3072


def column_block(axes, mine):
    column = lax.axis_index(axes) * mine
    start = pl.multiple_of((column >> 7) * LANES, LANES)
    return pl.ds(start, LANES), column & (LANES - 1)


def column_of(block, place):
    lane = lax.broadcasted_iota(jnp.int32, block.shape, 1)
    return jnp.sum(jnp.where(lane == place, block, 0).astype(jnp.float32), axis=1, keepdims=True).astype(jnp.int32)


def homes_of(table_v, cands_v, cands_s, rows_v, place):
    for k in range(cands_v.shape[0]):
        rows_v[k : k + 1, :] = table_v[pl.ds(cands_s[k, place] >> 7, 1), :]
    return column_of(rows_v[...], column_of(cands_v[...], place) & (LANES - 1))


def pack_kernel(held_items, axes, run, queries_ref, cands_ref, table_ref, send_ref, queries_v, table_v, cands_v, cands_s, rows_v, sems):
    devices, mine, width = send_ref.shape[0], queries_ref.shape[0], queries_ref.shape[1]
    per_query = cands_ref.shape[0]
    block, place = column_block(axes, mine)
    copies = [
        pltpu.make_async_copy(cands_ref.at[:, block], cands_s, sems.at[0]),
        pltpu.make_async_copy(cands_ref.at[:, block], cands_v, sems.at[1]),
        pltpu.make_async_copy(table_ref, table_v, sems.at[2]),
        pltpu.make_async_copy(queries_ref, queries_v, sems.at[3]),
    ]
    for copy in copies:
        copy.start()
    copies[3].wait()
    half = width // 2
    for start in range(0, devices, run):
        part = start // run % 2 * half
        send_ref[start : start + run, :, :half] = jnp.broadcast_to(queries_v[:, part : part + half][None], (run, mine, half))
    for copy in copies[:3]:
        copy.wait()
    lane = lax.broadcasted_iota(jnp.int32, (per_query, LANES), 1)
    order = lax.broadcasted_iota(jnp.int32, (per_query, LANES), 0)
    big = float(per_query * held_items)
    shift = held_items.bit_length() - 1
    digits = []
    for a in range(mine):
        home = homes_of(table_v, cands_v, cands_s, rows_v.at[a], place + a)
        key = (order * held_items + (home & (held_items - 1))).astype(jnp.float32)
        owned = home >> shift == lane
        first = jnp.min(jnp.where(owned, key, big), axis=0, keepdims=True)
        last = jnp.max(jnp.where(owned, key, -1.0), axis=0, keepdims=True)
        one = jnp.where(first < big, first.astype(jnp.int32) & (held_items - 1), -256)
        two = jnp.where(last > first, last.astype(jnp.int32) & (held_items - 1), -256)
        digits += [one >> 8, one & 255, two >> 8, two & 255]
    digits = [digit.astype(jnp.float32) for digit in digits]
    digits.append(jnp.zeros((LANES - len(digits), LANES), jnp.float32))
    digits = jnp.transpose(jnp.concatenate(digits, axis=0)).astype(send_ref.dtype)
    send_ref[:, :, half:] = jnp.broadcast_to(digits[:, None, :], (devices, mine, LANES))


def lookup_kernel(held_items, axes, mine, cands_ref, table_ref, probes_ref, list_home_ref, info_ref, table_v, cands_v, probes_v, list_home_v, cands_s, rows_v, sems):
    block, place = column_block(axes, mine)
    copies = [
        pltpu.make_async_copy(cands_ref.at[:, block], cands_s, sems.at[0]),
        pltpu.make_async_copy(cands_ref.at[:, block], cands_v, sems.at[1]),
        pltpu.make_async_copy(table_ref, table_v, sems.at[2]),
        pltpu.make_async_copy(probes_ref.at[:, block], probes_v, sems.at[3]),
        pltpu.make_async_copy(list_home_ref, list_home_v, sems.at[4]),
    ]
    for copy in copies:
        copy.start()
    for copy in copies:
        copy.wait()
    columns = [homes_of(table_v, cands_v, cands_s, rows_v.at[a], place + a) for a in range(mine)]
    for a in range(mine):
        ids = column_of(probes_v[...], place + a)
        stored = jnp.zeros_like(ids)
        for row in range(list_home_v.shape[0]):
            spread = jnp.broadcast_to(list_home_v[row : row + 1, :], (ids.shape[0], LANES))
            stored = stored + jnp.where(ids >> 7 == row, column_of(spread, ids & (LANES - 1)), 0)
        columns.append(stored)
    lane = lax.broadcasted_iota(jnp.int32, (LANES, LANES), 1)
    both = jnp.full((LANES, LANES), -1.0, jnp.float32)
    for j, column in enumerate(columns):
        column = column.astype(jnp.float32)
        short = jnp.full((LANES - column.shape[0], 1), -1.0, jnp.float32)
        both = jnp.where(lane == j, jnp.concatenate([column, short], axis=0), both)
    rows = jnp.transpose(both)[: 2 * mine, :].astype(jnp.int32)
    shift = held_items.bit_length() - 1
    per_query = cands_v.shape[0]
    before = lax.broadcasted_iota(jnp.int32, (per_query, LANES), 0) < lax.broadcasted_iota(
        jnp.int32, (per_query, LANES), 1
    )
    info = []
    for a in range(mine):
        owner = rows[a : a + 1, :] >> shift
        earlier = (columns[a] >> shift == owner) & before
        info += [owner, jnp.sum(earlier.astype(jnp.float32), axis=0, keepdims=True).astype(jnp.int32)]
        stored = rows[mine + a : mine + a + 1, :]
        info += [stored >> 1, stored & 1]
    info_ref[...] = jnp.concatenate(info, axis=0)


def scores(block, queries):
    return lax.dot_general(block, queries, (((1,), (1,)), ((), ())), preferred_element_type=jnp.float32)


def early_kernel(got_ref, lists_ref, items_ref, part_ref):
    count, half = got_ref.shape[0] * got_ref.shape[1], lists_ref.shape[2] // 2
    mine = got_ref[...].reshape(count, got_ref.shape[2])[:, :half]
    own = pl.ds(pl.multiple_of((lax.axis_index("row") & 1) * half, half), half)
    held_items = items_ref.shape[0]
    for start in range(0, held_items, CHUNK):
        part_ref[start : start + CHUNK, :] = scores(items_ref[start : start + CHUNK, own], mine)
    for start in range(0, EARLY, CHUNK):
        to = slice(held_items + start, held_items + start + CHUNK)
        part_ref[to, :] = scores(lists_ref[0, start : start + CHUNK, own], mine)


def score_kernel(scale, got_ref, other_ref, part_ref, lists_ref, items_ref, out_ref, wide_ref):
    width, held, list_rows = lists_ref.shape[2], lists_ref.shape[0], lists_ref.shape[1]
    count = got_ref.shape[0] * got_ref.shape[1]
    got = got_ref[...].reshape(count, got_ref.shape[2])
    other = other_ref[...].reshape(got.shape)
    half = width // 2
    mine, theirs = got[:, :half], other[:, :half]
    core = lax.axis_index("row") & 1
    queries = jnp.concatenate([jnp.where(core == 0, mine, theirs), jnp.where(core == 0, theirs, mine)], axis=1)
    rest = pl.ds(pl.multiple_of((1 - core) * half, half), half)
    digits = jnp.transpose(got[:, half:].astype(jnp.float32))
    odd = lax.broadcasted_iota(jnp.int32, (1, count), 1) & 1 == 1
    digits = jnp.where(odd, digits[4:8, :], digits[0:4, :])
    one = (digits[0:1, :] * 256.0 + digits[1:2, :]).astype(jnp.int32)
    two = (digits[2:3, :] * 256.0 + digits[3:4, :]).astype(jnp.int32)

    def fold(values):
        return jnp.sum(values.reshape(CHUNK // 8, 8, count), axis=0)

    results = []
    for i in range(held):
        total = jnp.zeros((8, count), jnp.float32)
        for start in range(0, list_rows, CHUNK):
            rows = slice(start, start + CHUNK)
            if i == 0 and start < EARLY:
                done = slice(items_ref.shape[0] + start, items_ref.shape[0] + start + CHUNK)
                found = part_ref[done, :] + scores(lists_ref[i, rows, rest], theirs)
            else:
                found = scores(lists_ref[i, rows, :], queries)
            positive = jnp.maximum(found, 0.0)
            total = total + fold(positive * positive)
        results.append(jnp.sum(total, axis=0, keepdims=True) * scale)
    first = second = jnp.zeros((8, count), jnp.float32)
    for start in range(0, items_ref.shape[0], CHUNK):
        rows = slice(start, start + CHUNK)
        found = part_ref[rows, :] + scores(items_ref[rows, rest], theirs)
        index = lax.broadcasted_iota(jnp.int32, (CHUNK, count), 0) + start
        first = first + fold(jnp.where(index == one, found, 0.0))
        second = second + fold(jnp.where(index == two, found, 0.0))
    results.append(jnp.sum(first, axis=0, keepdims=True))
    results.append(jnp.sum(second, axis=0, keepdims=True))
    results = jnp.concatenate(results, axis=0)
    results = jnp.concatenate([results, pltpu.roll(results, count - 1, 1)], axis=0)
    results = jnp.concatenate([results, jnp.zeros((LANES - results.shape[0], count), jnp.float32)], axis=0)
    wide_ref[...] = jnp.transpose(results)
    out_ref[...] = wide_ref[pl.ds(0, out_ref.shape[0], stride=2), :]


def in_vmem(array):
    return pltpu.with_memory_space_constraint(array, pltpu.VMEM)


def in_hbm(array):
    return pltpu.with_memory_space_constraint(array, pltpu.HBM)


def place_kernel(held_lists, back_ref, info_ref, mass_ref, rerank_ref):
    per_query, probed = rerank_ref.shape[1], mass_ref.shape[1]
    back = back_ref[...]
    row = lax.broadcasted_iota(jnp.int32, (back.shape[0], LANES), 0)

    def picked(at, a, j):
        owner, later = info_ref[4 * a + j : 4 * a + j + 1, :], info_ref[4 * a + j + 1 : 4 * a + j + 2, :]
        value = jnp.where(later > 0, back[:, at + 1 : at + 2], back[:, at : at + 1])
        return jnp.sum(jnp.where(row == owner, value, 0.0), axis=0, keepdims=True)

    for a in range(2):
        at = a * (held_lists + 2)
        rerank_ref[a : a + 1, :] = picked(at + held_lists, a, 0)[:, :per_query]
        mass_ref[a : a + 1, :] = picked(at, a, 2)[:, :probed]


def local(queries, lists, list_home, probes, initials, item_home, cands):
    devices = lax.axis_size(AXES)
    mine, width = queries.shape
    held_lists, list_rows = lists.shape[0], lists.shape[1]
    held_items = initials.shape[0]
    per_query, probed = cands.shape[1], probes.shape[1]
    scale = 1.0 / (width * list_rows)

    run = lax.axis_size("col")
    table = item_home.reshape(-1, LANES)
    send = pl.pallas_call(
        lambda *refs: pack_kernel(held_items, AXES, run, *refs),
        out_shape=pltpu.VMEM((devices, mine, width // 2 + LANES), queries.dtype),
        in_specs=[pl.BlockSpec(memory_space=pltpu.HBM)] * 3,
        out_specs=WHOLE,
        scratch_shapes=[
            pltpu.VMEM(queries.shape, queries.dtype),
            pltpu.VMEM((item_home.shape[0] // LANES, LANES), jnp.int32),
            pltpu.VMEM((per_query, LANES), jnp.int32),
            pltpu.SMEM((per_query, LANES), jnp.int32),
            pltpu.VMEM((mine, per_query, LANES), jnp.int32),
            pltpu.SemaphoreType.DMA((4,)),
        ],
        compiler_params=pltpu.CompilerParams(vmem_limit_bytes=4 * 1024 * 1024),
        cost_estimate=pl.CostEstimate(flops=1<<36, bytes_accessed=1<<28, transcendentals=0),
        name="pack",
    )(in_hbm(queries), in_hbm(cands.T), in_hbm(table))
    got = lax.all_to_all(send, AXES, 0, 0, tiled=True)
    pairs = [(i, i ^ 1) for i in range(lax.axis_size("row"))]
    other = lax.ppermute(got, "row", pairs)
    part = pl.pallas_call(
        early_kernel,
        out_shape=pltpu.VMEM((held_items + EARLY, devices * mine), jnp.float32),
        in_specs=[WHOLE] * 3,
        out_specs=WHOLE,
        compiler_params=pltpu.CompilerParams(vmem_limit_bytes=8 * 1024 * 1024),
        cost_estimate=pl.CostEstimate(
            flops=devices * mine * width * (held_items + EARLY),
            bytes_accessed=width * (held_items + EARLY), transcendentals=0,
        ),
        name="early",
    )(in_vmem(got), in_vmem(lists), in_vmem(initials))
    results = pl.pallas_call(
        lambda *refs: score_kernel(scale, *refs),
        out_shape=pltpu.VMEM((devices, LANES), jnp.float32),
        scratch_shapes=[pltpu.VMEM((devices * mine, LANES), jnp.float32)],
        in_specs=[WHOLE] * 5,
        out_specs=WHOLE,
        compiler_params=pltpu.CompilerParams(vmem_limit_bytes=16 * 1024 * 1024),
        cost_estimate=pl.CostEstimate(
            flops=2 * devices * mine * width * (held_lists * list_rows + held_items),
            bytes_accessed=2 * width * (held_lists * list_rows + held_items),
            transcendentals=0,
        ),
        name="score",
    )(in_vmem(got), in_vmem(other), in_vmem(part), in_vmem(lists), in_vmem(initials))
    results, table, late_cands, late_probes, homes = lax.optimization_barrier(
        (results, table, cands.T, probes.T, list_home.reshape(-1, LANES))
    )
    info = pl.pallas_call(
        lambda *refs: lookup_kernel(held_items, AXES, mine, *refs),
        out_shape=pltpu.VMEM((8, LANES), jnp.int32),
        in_specs=[pl.BlockSpec(memory_space=pltpu.HBM)] * 4,
        out_specs=WHOLE,
        scratch_shapes=[
            pltpu.VMEM(table.shape, jnp.int32),
            pltpu.VMEM((per_query, LANES), jnp.int32),
            pltpu.VMEM((probed, LANES), jnp.int32),
            pltpu.VMEM(homes.shape, jnp.int32),
            pltpu.SMEM((per_query, LANES), jnp.int32),
            pltpu.VMEM((mine, per_query, LANES), jnp.int32),
            pltpu.SemaphoreType.DMA((5,)),
        ],
        compiler_params=pltpu.CompilerParams(vmem_limit_bytes=4 * 1024 * 1024),
        cost_estimate=pl.CostEstimate(flops=0, bytes_accessed=2 * 1024 * 1024, transcendentals=0),
        name="lookup",
    )(in_hbm(late_cands), in_hbm(table), in_hbm(late_probes), in_hbm(homes))
    back = lax.all_to_all(results[:, None, :], AXES, 0, 0, tiled=True)[:, 0, :]
    return pl.pallas_call(
        lambda *refs: place_kernel(held_lists, *refs),
        out_shape=(
            jax.ShapeDtypeStruct((mine, probed), jnp.float32),
            jax.ShapeDtypeStruct((mine, per_query), jnp.float32),
        ),
        name="place",
    )(in_vmem(back), in_vmem(info))


def solution(mesh):
    return jax.shard_map(
        local,
        mesh=mesh,
        in_specs=(P(AXES, None), P(AXES, None, None), P(), P(), P(AXES, None), P(), P()),
        out_specs=(P(AXES, None), P(AXES, None)),
        check_vma=False,
    )
```

```python
import math

import jax
import jax.numpy as jnp
from jax import lax
from jax.experimental import pallas as pl
from jax.experimental.pallas import tpu as pltpu
from jax.sharding import PartitionSpec as P

AXES = ("row", "col")
LANES = 128
WHOLE = pl.BlockSpec(memory_space=pltpu.VMEM)
CHUNK = 1024
EARLY = 3072


def column_block(axes, mine):
    column = lax.axis_index(axes) * mine
    start = pl.multiple_of((column >> 7) * LANES, LANES)
    return pl.ds(start, LANES), column & (LANES - 1)


def column_of(block, place):
    lane = lax.broadcasted_iota(jnp.int32, block.shape, 1)
    return jnp.sum(jnp.where(lane == place, block, 0).astype(jnp.float32), axis=1, keepdims=True).astype(jnp.int32)


def homes_of(table_v, cands_v, cands_s, rows_v, place):
    for k in range(cands_v.shape[0]):
        rows_v[k : k + 1, :] = table_v[pl.ds(cands_s[k, place] >> 7, 1), :]
    return column_of(rows_v[...], column_of(cands_v[...], place) & (LANES - 1))


def pack_kernel(held_items, axes, run, queries_ref, cands_ref, table_ref, send_ref, queries_v, table_v, cands_v, cands_s, rows_v, sems):
    devices, mine, width = send_ref.shape[0], queries_ref.shape[0], queries_ref.shape[1]
    per_query = cands_ref.shape[0]
    block, place = column_block(axes, mine)
    copies = [
        pltpu.make_async_copy(cands_ref.at[:, block], cands_s, sems.at[0]),
        pltpu.make_async_copy(cands_ref.at[:, block], cands_v, sems.at[1]),
        pltpu.make_async_copy(table_ref, table_v, sems.at[2]),
        pltpu.make_async_copy(queries_ref, queries_v, sems.at[3]),
    ]
    for copy in copies:
        copy.start()
    copies[3].wait()
    half = width // 2
    for start in range(0, devices, run):
        part = start // run % 2 * half
        send_ref[start : start + run, :, :half] = jnp.broadcast_to(queries_v[:, part : part + half][None], (run, mine, half))
    for copy in copies[:3]:
        copy.wait()
    lane = lax.broadcasted_iota(jnp.int32, (per_query, LANES), 1)
    order = lax.broadcasted_iota(jnp.int32, (per_query, LANES), 0)
    big = float(per_query * held_items)
    shift = held_items.bit_length() - 1
    digits = []
    for a in range(mine):
        home = homes_of(table_v, cands_v, cands_s, rows_v.at[a], place + a)
        key = (order * held_items + (home & (held_items - 1))).astype(jnp.float32)
        owned = home >> shift == lane
        first = jnp.min(jnp.where(owned, key, big), axis=0, keepdims=True)
        last = jnp.max(jnp.where(owned, key, -1.0), axis=0, keepdims=True)
        one = jnp.where(first < big, first.astype(jnp.int32) & (held_items - 1), -256)
        two = jnp.where(last > first, last.astype(jnp.int32) & (held_items - 1), -256)
        digits += [one >> 8, one & 255, two >> 8, two & 255]
    digits = [digit.astype(jnp.float32) for digit in digits]
    digits.append(jnp.zeros((LANES - len(digits), LANES), jnp.float32))
    digits = jnp.transpose(jnp.concatenate(digits, axis=0)).astype(send_ref.dtype)
    send_ref[:, :, half:] = jnp.broadcast_to(digits[:, None, :], (devices, mine, LANES))


def lookup_kernel(held_items, axes, mine, cands_ref, table_ref, probes_ref, list_home_ref, info_ref, table_v, cands_v, probes_v, list_home_v, cands_s, rows_v, sems):
    block, place = column_block(axes, mine)
    copies = [
        pltpu.make_async_copy(cands_ref.at[:, block], cands_s, sems.at[0]),
        pltpu.make_async_copy(cands_ref.at[:, block], cands_v, sems.at[1]),
        pltpu.make_async_copy(table_ref, table_v, sems.at[2]),
        pltpu.make_async_copy(probes_ref.at[:, block], probes_v, sems.at[3]),
        pltpu.make_async_copy(list_home_ref, list_home_v, sems.at[4]),
    ]
    for copy in copies:
        copy.start()
    for copy in copies:
        copy.wait()
    columns = [homes_of(table_v, cands_v, cands_s, rows_v.at[a], place + a) for a in range(mine)]
    for a in range(mine):
        ids = column_of(probes_v[...], place + a)
        stored = jnp.zeros_like(ids)
        for row in range(list_home_v.shape[0]):
            spread = jnp.broadcast_to(list_home_v[row : row + 1, :], (ids.shape[0], LANES))
            stored = stored + jnp.where(ids >> 7 == row, column_of(spread, ids & (LANES - 1)), 0)
        columns.append(stored)
    lane = lax.broadcasted_iota(jnp.int32, (LANES, LANES), 1)
    both = jnp.full((LANES, LANES), -1.0, jnp.float32)
    for j, column in enumerate(columns):
        column = column.astype(jnp.float32)
        short = jnp.full((LANES - column.shape[0], 1), -1.0, jnp.float32)
        both = jnp.where(lane == j, jnp.concatenate([column, short], axis=0), both)
    rows = jnp.transpose(both)[: 2 * mine, :].astype(jnp.int32)
    shift = held_items.bit_length() - 1
    per_query = cands_v.shape[0]
    before = lax.broadcasted_iota(jnp.int32, (per_query, LANES), 0) < lax.broadcasted_iota(
        jnp.int32, (per_query, LANES), 1
    )
    info = []
    for a in range(mine):
        owner = rows[a : a + 1, :] >> shift
        earlier = (columns[a] >> shift == owner) & before
        info += [owner, jnp.sum(earlier.astype(jnp.float32), axis=0, keepdims=True).astype(jnp.int32)]
        stored = rows[mine + a : mine + a + 1, :]
        info += [stored >> 1, stored & 1]
    info_ref[...] = jnp.concatenate(info, axis=0)


def scores(block, queries):
    return lax.dot_general(block, queries, (((1,), (1,)), ((), ())), preferred_element_type=jnp.float32)


def early_kernel(got_ref, lists_ref, items_ref, part_ref):
    count, half = got_ref.shape[0] * got_ref.shape[1], lists_ref.shape[2] // 2
    mine = got_ref[...].reshape(count, got_ref.shape[2])[:, :half]
    own = pl.ds(pl.multiple_of((lax.axis_index("row") & 1) * half, half), half)
    held_items = items_ref.shape[0]
    for start in range(0, held_items, CHUNK):
        part_ref[start : start + CHUNK, :] = scores(items_ref[start : start + CHUNK, own], mine)
    for start in range(0, EARLY, CHUNK):
        to = slice(held_items + start, held_items + start + CHUNK)
        part_ref[to, :] = scores(lists_ref[0, start : start + CHUNK, own], mine)


def score_kernel(scale, got_ref, other_ref, part_ref, lists_ref, items_ref, out_ref, wide_ref):
    width, held, list_rows = lists_ref.shape[2], lists_ref.shape[0], lists_ref.shape[1]
    count = got_ref.shape[0] * got_ref.shape[1]
    got = got_ref[...].reshape(count, got_ref.shape[2])
    other = other_ref[...].reshape(got.shape)
    half = width // 2
    mine, theirs = got[:, :half], other[:, :half]
    core = lax.axis_index("row") & 1
    queries = jnp.concatenate([jnp.where(core == 0, mine, theirs), jnp.where(core == 0, theirs, mine)], axis=1)
    rest = pl.ds(pl.multiple_of((1 - core) * half, half), half)
    digits = jnp.transpose(got[:, half:].astype(jnp.float32)[:, :8])
    odd = lax.broadcasted_iota(jnp.int32, (1, count), 1) & 1 == 1
    digits = jnp.where(odd, digits[4:8, :], digits[0:4, :])
    one = (digits[0:1, :] * 256.0 + digits[1:2, :]).astype(jnp.int32)
    two = (digits[2:3, :] * 256.0 + digits[3:4, :]).astype(jnp.int32)

    def fold(values):
        return jnp.sum(values.reshape(CHUNK // 8, 8, count), axis=0)

    results = []
    for i in range(held):
        total = jnp.zeros((8, count), jnp.float32)
        for start in range(0, list_rows, CHUNK):
            rows = slice(start, start + CHUNK)
            if i == 0 and start < EARLY:
                done = slice(items_ref.shape[0] + start, items_ref.shape[0] + start + CHUNK)
                found = part_ref[done, :] + scores(lists_ref[i, rows, rest], theirs)
            else:
                found = scores(lists_ref[i, rows, :], queries)
            positive = jnp.maximum(found, 0.0)
            total = total + fold(positive * positive)
        results.append(jnp.sum(total, axis=0, keepdims=True) * scale)
    first = second = jnp.zeros((8, count), jnp.float32)
    for start in range(0, items_ref.shape[0], CHUNK):
        rows = slice(start, start + CHUNK)
        found = part_ref[rows, :] + scores(items_ref[rows, rest], theirs)
        index = lax.broadcasted_iota(jnp.int32, (CHUNK, count), 0) + start
        first = first + fold(jnp.where(index == one, found, 0.0))
        second = second + fold(jnp.where(index == two, found, 0.0))
    results.append(jnp.sum(first, axis=0, keepdims=True))
    results.append(jnp.sum(second, axis=0, keepdims=True))
    results = jnp.concatenate(results, axis=0)
    results = jnp.concatenate([results, pltpu.roll(results, count - 1, 1)], axis=0)
    wide_ref[:, : results.shape[0]] = jnp.transpose(results)
    wide_ref[:, results.shape[0] :] = jnp.zeros((count, LANES - results.shape[0]), jnp.float32)
    out_ref[...] = wide_ref[pl.ds(0, out_ref.shape[0], stride=2), :]


def in_vmem(array):
    return pltpu.with_memory_space_constraint(array, pltpu.VMEM)


def in_hbm(array):
    return pltpu.with_memory_space_constraint(array, pltpu.HBM)


def place_kernel(held_lists, back_ref, info_ref, mass_ref, rerank_ref):
    per_query, probed = rerank_ref.shape[1], mass_ref.shape[1]
    back = back_ref[...]
    row = lax.broadcasted_iota(jnp.int32, (back.shape[0], LANES), 0)

    def picked(at, a, j):
        owner, later = info_ref[4 * a + j : 4 * a + j + 1, :], info_ref[4 * a + j + 1 : 4 * a + j + 2, :]
        value = jnp.where(later > 0, back[:, at + 1 : at + 2], back[:, at : at + 1])
        return jnp.sum(jnp.where(row == owner, value, 0.0), axis=0, keepdims=True)

    for a in range(2):
        at = a * (held_lists + 2)
        rerank_ref[a : a + 1, :] = picked(at + held_lists, a, 0)[:, :per_query]
        mass_ref[a : a + 1, :] = picked(at, a, 2)[:, :probed]


def local(queries, lists, list_home, probes, initials, item_home, cands):
    devices = lax.axis_size(AXES)
    mine, width = queries.shape
    held_lists, list_rows = lists.shape[0], lists.shape[1]
    held_items = initials.shape[0]
    per_query, probed = cands.shape[1], probes.shape[1]
    scale = 1.0 / (width * list_rows)

    run = lax.axis_size("col")
    table = item_home.reshape(-1, LANES)
    send = pl.pallas_call(
        lambda *refs: pack_kernel(held_items, AXES, run, *refs),
        out_shape=pltpu.VMEM((devices, mine, width // 2 + LANES), queries.dtype),
        in_specs=[pl.BlockSpec(memory_space=pltpu.HBM)] * 3,
        out_specs=WHOLE,
        scratch_shapes=[
            pltpu.VMEM(queries.shape, queries.dtype),
            pltpu.VMEM((item_home.shape[0] // LANES, LANES), jnp.int32),
            pltpu.VMEM((per_query, LANES), jnp.int32),
            pltpu.SMEM((per_query, LANES), jnp.int32),
            pltpu.VMEM((mine, per_query, LANES), jnp.int32),
            pltpu.SemaphoreType.DMA((4,)),
        ],
        compiler_params=pltpu.CompilerParams(vmem_limit_bytes=4 * 1024 * 1024),
        cost_estimate=pl.CostEstimate(flops=1<<36, bytes_accessed=1<<28, transcendentals=0),
        name="pack",
    )(in_hbm(queries), in_hbm(cands.T), in_hbm(table))
    got = lax.all_to_all(send, AXES, 0, 0, tiled=True)
    pairs = [(i, i ^ 1) for i in range(lax.axis_size("row"))]
    other = lax.ppermute(got, "row", pairs)
    part = pl.pallas_call(
        early_kernel,
        out_shape=pltpu.VMEM((held_items + EARLY, devices * mine), jnp.float32),
        in_specs=[WHOLE] * 3,
        out_specs=WHOLE,
        compiler_params=pltpu.CompilerParams(vmem_limit_bytes=8 * 1024 * 1024),
        cost_estimate=pl.CostEstimate(
            flops=devices * mine * width * (held_items + EARLY),
            bytes_accessed=width * (held_items + EARLY), transcendentals=0,
        ),
        name="early",
    )(in_vmem(got), in_vmem(lists), in_vmem(initials))
    results = pl.pallas_call(
        lambda *refs: score_kernel(scale, *refs),
        out_shape=pltpu.VMEM((devices, LANES), jnp.float32),
        scratch_shapes=[pltpu.VMEM((devices * mine, LANES), jnp.float32)],
        in_specs=[WHOLE] * 5,
        out_specs=WHOLE,
        compiler_params=pltpu.CompilerParams(vmem_limit_bytes=16 * 1024 * 1024),
        cost_estimate=pl.CostEstimate(
            flops=2 * devices * mine * width * (held_lists * list_rows + held_items),
            bytes_accessed=2 * width * (held_lists * list_rows + held_items),
            transcendentals=0,
        ),
        name="score",
    )(in_vmem(got), in_vmem(other), in_vmem(part), in_vmem(lists), in_vmem(initials))
    results, table, late_cands, late_probes, homes = lax.optimization_barrier(
        (results, table, cands.T, probes.T, list_home.reshape(-1, LANES))
    )
    info = pl.pallas_call(
        lambda *refs: lookup_kernel(held_items, AXES, mine, *refs),
        out_shape=pltpu.VMEM((8, LANES), jnp.int32),
        in_specs=[pl.BlockSpec(memory_space=pltpu.HBM)] * 4,
        out_specs=WHOLE,
        scratch_shapes=[
            pltpu.VMEM(table.shape, jnp.int32),
            pltpu.VMEM((per_query, LANES), jnp.int32),
            pltpu.VMEM((probed, LANES), jnp.int32),
            pltpu.VMEM(homes.shape, jnp.int32),
            pltpu.SMEM((per_query, LANES), jnp.int32),
            pltpu.VMEM((mine, per_query, LANES), jnp.int32),
            pltpu.SemaphoreType.DMA((5,)),
        ],
        compiler_params=pltpu.CompilerParams(vmem_limit_bytes=4 * 1024 * 1024),
        cost_estimate=pl.CostEstimate(flops=0, bytes_accessed=2 * 1024 * 1024, transcendentals=0),
        name="lookup",
    )(in_hbm(late_cands), in_hbm(table), in_hbm(late_probes), in_hbm(homes))
    back = lax.all_to_all(results[:, None, :], AXES, 0, 0, tiled=True)[:, 0, :]
    return pl.pallas_call(
        lambda *refs: place_kernel(held_lists, *refs),
        out_shape=(
            jax.ShapeDtypeStruct((mine, probed), jnp.float32),
            jax.ShapeDtypeStruct((mine, per_query), jnp.float32),
        ),
        name="place",
    )(in_vmem(back), in_vmem(info))


def solution(mesh):
    return jax.shard_map(
        local,
        mesh=mesh,
        in_specs=(P(AXES, None), P(AXES, None, None), P(), P(), P(AXES, None), P(), P()),
        out_specs=(P(AXES, None), P(AXES, None)),
        check_vma=False,
    )
```
